256 devices in a mesh: rows: 32 (over z, y), grp: 8 (over x, core).
Axes of the slice: x: 4, y: 4, z: 8, core: 2. Of those that a mesh axis runs over, the one named last changes fastest.
Arguments:
- activations: bfloat16 [24576, 8192], P(('rows', 'grp')), may hold values from 0 to 1
- weight_tiles: bfloat16 [3, 512, 2, 128, 128], P(None, ('rows', 'grp')), may hold values from -0.75 to 0.75
- tile_index: int32 [3, 512, 1], replicated, may hold values from 0 to 511, as said below
- bias_terms: float32 [3, 65536], replicated, may hold values from -0.3 to 0.3
- demand: int32 [256, 64], P(('rows', 'grp')), may hold values from 0 to 511, as said below
Outputs:
- final_acts: bfloat16 [24576, 8192], P(('rows', 'grp'))
The draws below stay inside these ranges and needn't reach their ends.
Inputs may be any that keep to these rules, and one draw needn't show every extreme that they name: Each row of demand lists 64 distinct blocks made of whole groups [g * 4, (g + 1) * 4); every range [r * 16, (r + 1) * 16) holds either none of them or exactly one group of 4. tile_index[l, b, k] is a block of b's own group [(b // 4) * 4, (b // 4 + 1) * 4), never b itself.
All inputs are finite; a program needn't handle non-finite values.
Results may differ from the reference program's by a relative error of at most 0.0057.
Values may be sent and summed in bfloat16 or wider, within the bound.
No kernel may reach another device: no remote copies, remote signals or barrier semaphores. Data moves between devices by JAX's collectives and lax.ppermute only.
A program may use at most 128 MiB of HBM per device.

```python
import jax
import jax.numpy as jnp
from jax import lax

NEURONS = 65536
TILE = 128
NB = 512
LAYERS = 3
K_OFF = 1
CAP = 4
BPR = 16
LIVE = 64
R_DEV = 96
TOTAL_ROWS = 24576
N_ROWS = 32
DEVICES = 256


def draw_tile_index(key, part):
    block_count = NEURONS // TILE
    offsets = jax.random.randint(jax.random.fold_in(key, 11), (LAYERS, block_count, K_OFF), 1, CAP).astype(jnp.int32)
    blocks = jnp.arange(block_count, dtype=jnp.int32)[None, :, None]
    members = (blocks % CAP + offsets) % CAP
    return (blocks // CAP * CAP + members).astype(jnp.int32)


def draw_demand(key, part):

    def one_device(dev_key):
        key_range, key_group, key_order = jax.random.split(dev_key, 3)
        ranges = jax.random.permutation(key_range, N_ROWS)[:N_ROWS // 2].astype(jnp.int32)
        groups = jax.random.randint(key_group, (N_ROWS // 2,), 0, BPR // CAP).astype(jnp.int32)
        starts = ranges * BPR + groups * CAP
        blocks = (starts[:, None] + jnp.arange(CAP, dtype=jnp.int32)[None, :]).reshape(-1)
        return jax.random.permutation(key_order, blocks).astype(jnp.int32)
    return jax.vmap(one_device)(jax.random.split(jax.random.fold_in(key, 23), DEVICES))


def shard_levels(rng, extent, shards, smallest, high):
    def one(axis_at, shards_of):
        heights = jax.random.uniform(jax.random.fold_in(jax.random.fold_in(rng, 6), axis_at), (shards_of,), jnp.float32, smallest / len(shards), high / len(shards))
        return jnp.repeat(jnp.exp(heights), extent[axis_at] // shards_of).reshape((-1,) + (1,) * (len(extent) - axis_at - 1))

    factor_of = one(*shards[0])
    for cut in shards[1:]:
        factor_of = factor_of * one(*cut)
    return factor_of


def bell_draw(rng, dims, scale, bound, shards=(), kind=jnp.bfloat16):
    gain = shard_levels(rng, dims, shards, -0.22, 0.18) if shards else 1.0
    array = jax.random.normal(rng, dims, jnp.float32) * scale * gain
    return jnp.minimum(jnp.maximum(array, -bound), bound).astype(kind)


def setup_inputs(seed: int = 0) -> dict:
    key_of = jax.random.split(jax.random.key(seed), 6)
    activations = jnp.clip(1.0 * jax.random.uniform(key_of[0], (TOTAL_ROWS, LIVE * TILE), jnp.float32) ** shard_levels(key_of[0], (TOTAL_ROWS, LIVE * TILE), ((0, 256),), -0.2, 0.2), 0.0, 1.0).astype(jnp.bfloat16)
    weight_tiles = bell_draw(key_of[1], (LAYERS, NB, 1 + K_OFF, TILE, TILE), (TILE // 2) ** -0.5, 0.75, ((1, 256),))
    tile_index = draw_tile_index(jax.random.fold_in(key_of[5], 71), 0)
    bias_terms = jnp.clip(jax.random.uniform(key_of[3], (LAYERS, NEURONS), jnp.float32, -0.3, 0.3), -0.3, 0.3)
    demand = draw_demand(jax.random.fold_in(key_of[5], 71), 0)
    return {"activations": activations, "weight_tiles": weight_tiles, "tile_index": tile_index, "bias_terms": bias_terms, "demand": demand}


def reference(activations, weight_tiles, tile_index, bias_terms, demand):
    block_count = NEURONS // TILE
    acts = activations.reshape(DEVICES, R_DEV, LIVE, TILE)
    bias_blocks = bias_terms.reshape(LAYERS, block_count, TILE)

    def one_device(inputs):
        current, live_blocks = inputs
        for layer_num in range(LAYERS):
            weights = weight_tiles[layer_num][live_blocks].astype(jnp.float32)
            off_blocks = tile_index[layer_num][live_blocks]
            matches = (off_blocks[:, :, None] == live_blocks[None, None, :]).astype(jnp.float32)
            chosen = jnp.einsum('ikp,rpt->rikt', matches, current.astype(jnp.float32))
            diag_part = jnp.einsum('rit,itu->riu', current.astype(jnp.float32), weights[:, 0])
            off_part = jnp.einsum('rikt,iktu->riu', chosen, weights[:, 1:])
            pre_act = diag_part + off_part + bias_blocks[layer_num][live_blocks][None]
            current = jax.nn.relu(pre_act).astype(jnp.bfloat16)
        return current

    result = lax.map(one_device, (acts, demand))
    return result.reshape(DEVICES * R_DEV, LIVE * TILE)
```

```python
import jax
import jax.numpy as jnp
from jax import lax
from jax.experimental import pallas as pl
from jax.experimental.pallas import tpu as pltpu
from jax.sharding import Mesh
from jax.sharding import PartitionSpec as P

LAYERS = 3
CAP = 4
NZ, NY, NX, NC = 8, 4, 4, 2
AXES = ("z", "y", "x", "c")
PLACES = [(z, y, x, c) for z in range(NZ) for y in range(NY) for x in range(NX) for c in range(NC)]
PLACE_ID = {place: i for i, place in enumerate(PLACES)}
MOVES = [(dz, dy) for dz in (0, 1, 3, 2) for dy in (0, 1, 3, 2)]
ROWS = 96
BLOCK = 128
SLOT_ROWS = CAP * ROWS
TAG_ROWS = 16
SENT_ROWS = 2 * SLOT_ROWS + TAG_ROWS
VMEM_LIMIT = 40 * 1024 * 1024


def signed(step, c):
    return {0: 0, 1: 1, 3: -1, 2: 2 - 4 * c}[step]


def permute(value, target):
    pairs = [(PLACE_ID[p], PLACE_ID[target(*p)]) for p in PLACES]
    return lax.ppermute(value, AXES, pairs)


def send(value, move, back):
    sign = -1 if back else 1

    def target(z, y, x, c):
        dz, dy = signed(move[0], c), signed(move[1], c)
        return ((z + sign * dz) % NZ, (y + sign * dy) % NY, x, c)

    return value if move == (0, 0) else permute(value, target)


def shifted(value, dz=0, dx=0, dc=0):
    return permute(value, lambda z, y, x, c: ((z + dz) % NZ, y, (x + dx) % NX, (c + dc) % NC))


def slot_range(device, move, h):
    z, y, c = device // 32, (device // 8) % 4, device % 2

    def step(s):
        return {0: 0, 1: 1, 3: 7, 2: 2 + 4 * c}[s]

    return ((z + step(move[0]) + 4 * h) % NZ) * NY + (y + step(move[1])) % NY


def note_places(demand, place, group):
    for r in range(NZ * NY):
        group[r] = -1
    for p in range(demand.shape[1]):
        block = demand[0, p]
        place[(block // 16) * CAP + block % CAP] = p
        group[block // 16] = (block // CAP) % 4


def pack_kernel(device, demand, acts, *rest):
    outs, (place, group) = rest[: len(MOVES)], rest[len(MOVES) :]
    note_places(demand, place, group)
    for i, move in enumerate(MOVES):
        tags = []
        for h in range(2):
            r = slot_range(device[0], move, h)
            tags.append(group[r])

            @pl.when(group[r] >= 0)
            def _():
                for k in range(CAP):
                    col = pl.multiple_of(place[r * CAP + k] * BLOCK, BLOCK)
                    outs[i][pl.ds(h * SLOT_ROWS + k * ROWS, ROWS), :] = acts[:, pl.ds(col, BLOCK)]

        line = lax.broadcasted_iota(jnp.int32, (TAG_ROWS, BLOCK), 0)
        tag = jnp.where(line < 8, tags[0], tags[1]).astype(jnp.float32)
        outs[i][pl.ds(2 * SLOT_ROWS, TAG_ROWS), :] = tag.astype(jnp.bfloat16)


def unpack_kernel(device, demand, *rest):
    ins, (out, place, group) = rest[: len(MOVES)], rest[len(MOVES) :]
    note_places(demand, place, group)
    for i, move in enumerate(MOVES):
        for h in range(2):
            r = slot_range(device[0], move, h)

            @pl.when(group[r] >= 0)
            def _():
                for k in range(CAP):
                    col = pl.multiple_of(place[r * CAP + k] * BLOCK, BLOCK)
                    out[:, pl.ds(col, BLOCK)] = ins[i][pl.ds(h * SLOT_ROWS + k * ROWS, ROWS), :]


def layers_kernel(count, device, members, biases, home, mine, other, *rest):
    ins, outs, (partner, state, sems) = rest[:count], rest[count : 2 * count], rest[2 * count :]
    x, c = (device[0] // 2) % 4, device[0] % 2
    copies = [
        pltpu.make_async_copy(mine, partner.at[c], sems.at[0]),
        pltpu.make_async_copy(other, partner.at[1 - c], sems.at[1]),
    ]
    for copy in copies:
        copy.start()
    for copy in copies:
        copy.wait()
    tags = []
    for i in range(count):
        tag = ins[i][pl.ds(2 * SLOT_ROWS, TAG_ROWS), :].astype(jnp.float32)
        tags.append([jnp.max(tag[8 * h : 8 * h + 8]).astype(jnp.int32) for h in range(2)])
    for i in range(count):
        for h in range(2):
            group = tags[i][h]
            base = h * SLOT_ROWS

            @pl.when(group >= 0)
            def _():
                for layer in range(LAYERS):
                    src, at = (ins[i], base) if layer == 0 else (state.at[layer % 2], 0)
                    for k in range(CAP):
                        block = group * CAP + k
                        peer = members[h, layer, block]
                        own = src[pl.ds(at + k * ROWS, ROWS), :]
                        off = src[pl.ds(pl.multiple_of(at + peer * ROWS, 16), ROWS), :]
                        if h == 0:
                            weights = home[layer, block]
                        else:
                            weights = partner[k // 2, (group - x) % 4, layer, k % 2]
                        total = jnp.dot(
                            jnp.concatenate([own, off], axis=1), weights, preferred_element_type=jnp.float32
                        )
                        total = total + biases[h, layer, pl.ds(block, 1), :]
                        new = jnp.maximum(total, 0).astype(jnp.bfloat16)
                        if layer == LAYERS - 1:
                            outs[i][pl.ds(base + k * ROWS, ROWS), :] = new
                        else:
                            state[(layer + 1) % 2, pl.ds(k * ROWS, ROWS), :] = new


SMEM = pl.BlockSpec(memory_space=pltpu.SMEM)
VMEM = pl.BlockSpec(memory_space=pltpu.VMEM)
ANY = pl.BlockSpec(memory_space=pl.ANY)
PARAMS = pltpu.CompilerParams(vmem_limit_bytes=VMEM_LIMIT)
PLACE_SCRATCH = [pltpu.SMEM((128,), jnp.int32), pltpu.SMEM((32,), jnp.int32)]


def shards(activations, weight_tiles, tile_index, bias_terms, demand):
    device = lax.axis_index(AXES).astype(jnp.int32).reshape(1)
    sent = jax.ShapeDtypeStruct((SENT_ROWS, BLOCK), jnp.bfloat16)
    done = jax.ShapeDtypeStruct((2 * SLOT_ROWS, BLOCK), jnp.bfloat16)

    home = lax.all_gather(weight_tiles, ("x", "c"), axis=1, tiled=True).reshape(LAYERS, 16, 256, 128)
    near = shifted(weight_tiles.reshape(LAYERS, 2, 256, 128), dz=4)
    mine = jnp.stack([near, shifted(near, dx=-1), shifted(near, dx=2), shifted(near, dx=1)])
    other = shifted(mine, dc=1)

    outgoing = pl.pallas_call(
        pack_kernel,
        out_shape=[sent] * len(MOVES),
        in_specs=[SMEM, SMEM, VMEM],
        out_specs=[VMEM] * len(MOVES),
        scratch_shapes=PLACE_SCRATCH,
        compiler_params=PARAMS,
        name="pack",
    )(device, demand, activations)
    arrived = [send(v, move, False) for v, move in zip(outgoing, MOVES)]

    own_range = lax.axis_index(("z", "y"))
    ranges = [own_range, (own_range + NZ * NY // 2) % (NZ * NY)]
    members = jnp.stack(
        [lax.dynamic_slice_in_dim(tile_index[:, :, 0], r * 16, 16, 1) % CAP for r in ranges]
    )
    biases = jnp.stack(
        [lax.dynamic_slice_in_dim(bias_terms, r * 16 * BLOCK, 16 * BLOCK, 1).reshape(LAYERS, 16, BLOCK) for r in ranges]
    )

    returned = [None] * len(MOVES)
    for part in (range(0, 8), range(8, 16)):
        count = len(part)
        results = pl.pallas_call(
            lambda *refs, count=count: layers_kernel(count, *refs),
            out_shape=[done] * count,
            in_specs=[SMEM, SMEM, VMEM, VMEM, ANY, ANY] + [VMEM] * count,
            out_specs=[VMEM] * count,
            scratch_shapes=[
                pltpu.VMEM((2, 4, LAYERS, 2, 256, 128), jnp.bfloat16),
                pltpu.VMEM((2, SLOT_ROWS, BLOCK), jnp.bfloat16),
                pltpu.SemaphoreType.DMA((2,)),
            ],
            compiler_params=PARAMS,
            name="layers",
        )(device, members, biases, home, mine, other, *[arrived[i] for i in part])
        for i, value in zip(part, results):
            returned[i] = send(value, MOVES[i], True)

    return pl.pallas_call(
        unpack_kernel,
        out_shape=jax.ShapeDtypeStruct(activations.shape, activations.dtype),
        in_specs=[SMEM, SMEM] + [VMEM] * len(MOVES),
        out_specs=VMEM,
        scratch_shapes=PLACE_SCRATCH,
        compiler_params=PARAMS,
        name="unpack",
    )(device, demand, *returned)


def solution(mesh):
    finer = Mesh(mesh.devices.reshape(NZ, NY, NX, NC), AXES)
    placed = (P(AXES, None), P(None, AXES, None, None, None), P(), P(), P(AXES, None))
    return jax.shard_map(
        shards, mesh=finer, in_specs=placed, out_specs=P(AXES, None), check_vma=False
    )
```

```python
import jax
import jax.numpy as jnp
from jax import lax
from jax.experimental import pallas as pl
from jax.experimental.pallas import tpu as pltpu
from jax.sharding import Mesh
from jax.sharding import PartitionSpec as P

LAYERS = 3
CAP = 4
NZ, NY, NX, NC = 8, 4, 4, 2
AXES = ("z", "y", "x", "c")
PLACES = [(z, y, x, c) for z in range(NZ) for y in range(NY) for x in range(NX) for c in range(NC)]
PLACE_ID = {place: i for i, place in enumerate(PLACES)}
MOVES = [
    *((0, 1), (0, 3), (0, 2), (1, 2), (3, 2)),
    *((1, 1), (3, 3), (2, 2), (1, 3), (3, 1)),
    *((2, 1), (2, 3), (1, 0), (3, 0), (2, 0), (0, 0)),
]
ROWS = 96
BLOCK = 128
SLOT_ROWS = CAP * ROWS
TAG_ROWS = 16
SENT_ROWS = 2 * SLOT_ROWS + TAG_ROWS
WIDTH = 4
PARTS = [[5, 6, 7, 8, 9], [10, 11, 12, 13, 14, 0, 1, 2, 3, 4, 15]]


def signed(step, c):
    return {0: 0, 1: 1, 3: -1, 2: 2 - 4 * c}[step]


def permute(value, target):
    pairs = [(PLACE_ID[p], PLACE_ID[target(*p)]) for p in PLACES]
    return lax.ppermute(value, AXES, pairs)


def send(value, move, back):
    sign = -1 if back else 1

    def target(z, y, x, c):
        dz, dy = signed(move[0], c), signed(move[1], c)
        return ((z + sign * dz) % NZ, (y + sign * dy) % NY, x, c)

    return value if move == (0, 0) else permute(value, target)


def shifted(value, dz=0, dx=0, dc=0):
    return permute(value, lambda z, y, x, c: ((z + dz) % NZ, y, (x + dx) % NX, (c + dc) % NC))


def slot_range(device, move, h):
    z, y, c = device // 32, (device // 8) % 4, device % 2

    def step(s):
        return {0: 0, 1: 1, 3: 7, 2: 2 + 4 * c}[s]

    return ((z + step(move[0]) + 4 * h) % NZ) * NY + (y + step(move[1])) % NY


def note_places(demand, place, group):
    for r in range(NZ * NY):
        group[r] = -1
    for p in range(demand.shape[1]):
        block = demand[0, p]
        place[(block // 16) * CAP + block % CAP] = p
        group[block // 16] = (block // CAP) % 4


def bundle_slots(device, place, group):
    for i, move in enumerate(MOVES):
        for h in range(2):
            r = slot_range(device, move, h)
            yield i, h, r, group[r]


def pack_kernel(device, demand, tiles, acts, tiles_out, *rest):
    outs, (place, group, tags, sems) = rest[: len(MOVES)], rest[len(MOVES) :]
    handed_on = pltpu.make_async_copy(tiles, tiles_out, sems.at[0])
    handed_on.start()
    note_places(demand, place, group)
    found = [[None, None] for _ in MOVES]
    for i, h, r, live in bundle_slots(device[0], place, group):
        found[i][h] = live

        @pl.when(live >= 0)
        def _():
            for k in range(CAP):
                col = pl.multiple_of(place[r * CAP + k] * BLOCK, BLOCK)
                block = outs[i].at[pl.ds(h * SLOT_ROWS + k * ROWS, ROWS), :]
                pltpu.make_async_copy(acts.at[:, pl.ds(col, BLOCK)], block, sems.at[1]).start()

    line = lax.broadcasted_iota(jnp.int32, (TAG_ROWS, BLOCK), 0)
    tag_copies = []
    for i in range(len(MOVES)):
        tag = jnp.where(line < 8, found[i][0], found[i][1]).astype(jnp.float32)
        tags[i] = tag.astype(jnp.bfloat16)
        tag_copies.append(
            pltpu.make_async_copy(tags.at[i], outs[i].at[pl.ds(2 * SLOT_ROWS, TAG_ROWS), :], sems.at[2 + i])
        )
        tag_copies[-1].start()
    for copy in tag_copies:
        copy.wait()
    handed_on.wait()
    pltpu.make_async_copy(acts, acts, sems.at[1]).wait()


def unpack_kernel(device, demand, *rest):
    ins, (out, place, group, sem) = rest[: len(MOVES)], rest[len(MOVES) :]
    note_places(demand, place, group)
    for i, h, r, live in bundle_slots(device[0], place, group):

        @pl.when(live >= 0)
        def _():
            for k in range(CAP):
                col = pl.multiple_of(place[r * CAP + k] * BLOCK, BLOCK)
                block = ins[i].at[pl.ds(h * SLOT_ROWS + k * ROWS, ROWS), :]
                pltpu.make_async_copy(block, out.at[:, pl.ds(col, BLOCK)], sem).start()

    pltpu.make_async_copy(out, out, sem).wait()


def layers_kernel(count, members, biases, home, partner, *rest):
    ins, outs, rest = rest[:count], rest[count : 2 * count], rest[2 * count :]
    weights, slots, tags, queue, groups, sems, *states = rest
    firsts, seconds = states[:WIDTH], states[WIDTH:]
    spare = 2 * count
    copies = []
    for i in range(count):
        copies.append(
            pltpu.make_async_copy(ins[i].at[pl.ds(2 * SLOT_ROWS, TAG_ROWS), :], tags.at[i], sems.at[i])
        )
    for h, source in enumerate((home, partner)):
        copies.append(pltpu.make_async_copy(source, weights.at[h], sems.at[count + h]))
    for i in range(count):
        for h in range(2):
            s = 2 * i + h
            block = ins[i].at[pl.ds(h * SLOT_ROWS, SLOT_ROWS), :]
            copies.append(pltpu.make_async_copy(block, slots.at[s], sems.at[count + 2 + s]))
    for copy in copies:
        copy.start()
    for copy in copies[:count]:
        copy.wait()
    found = []
    for i in range(count):
        tag = tags[i].astype(jnp.float32)
        found += [jnp.max(tag[8 * h : 8 * h + 8]).astype(jnp.int32) for h in range(2)]
    live = jnp.int32(0)
    for s in range(2 * count):
        queue[live] = s
        groups[s] = jnp.maximum(found[s], 0)
        live = live + (found[s] >= 0).astype(jnp.int32)
    groups[spare] = 0
    for u in range(WIDTH):
        queue[live + u] = spare
    for copy in copies[count:]:
        copy.wait()

    def several(turn, carry):
        picked = [queue[turn * WIDTH + u] for u in range(WIDTH)]
        group = [groups[s] for s in picked]
        side = [lax.rem(s, 2) for s in picked]
        for layer in range(LAYERS):
            for u in range(WIDTH):
                src = (slots.at[picked[u]], firsts[u], seconds[u])[layer]
                dst = (firsts[u], seconds[u], slots.at[picked[u]])[layer]
                for k in range(CAP):
                    block = group[u] * CAP + k
                    peer = members[side[u], layer, block]
                    own = src[pl.ds(k * ROWS, ROWS), :]
                    off = src[pl.ds(pl.multiple_of(peer * ROWS, 16), ROWS), :]
                    total = jnp.dot(
                        jnp.concatenate([own, off], axis=1),
                        weights[side[u], layer, block],
                        preferred_element_type=jnp.float32,
                    )
                    total = total + biases[side[u], layer, pl.ds(block, 1), :]
                    dst[pl.ds(k * ROWS, ROWS), :] = jnp.maximum(total, 0).astype(jnp.bfloat16)
        return carry

    lax.fori_loop(0, (live + WIDTH - 1) // WIDTH, several, 0)
    copies = []
    for i in range(count):
        for h in range(2):
            s = 2 * i + h
            block = outs[i].at[pl.ds(h * SLOT_ROWS, SLOT_ROWS), :]
            copies.append(pltpu.make_async_copy(slots.at[s], block, sems.at[count + 2 + s]))
    for copy in copies:
        copy.start()
    for copy in copies:
        copy.wait()


SMEM = pl.BlockSpec(memory_space=pltpu.SMEM)
VMEM = pl.BlockSpec(memory_space=pltpu.VMEM)
HBM = pl.BlockSpec(memory_space=pltpu.HBM)
PLACE_SCRATCH = [pltpu.SMEM((128,), jnp.int32), pltpu.SMEM((32,), jnp.int32)]


def cost(microseconds):
    return pl.CostEstimate(flops=0, bytes_accessed=int(microseconds * 3e6), transcendentals=0)


def grant(mebibytes):
    return pltpu.CompilerParams(vmem_limit_bytes=mebibytes * 1024 * 1024)


def in_hbm(value):
    return pltpu.with_memory_space_constraint(value, pltpu.HBM)


def after(value, *others):
    return pl.pallas_call(
        lambda *refs: None,
        out_shape=jax.ShapeDtypeStruct(value.shape, value.dtype),
        in_specs=[HBM] * (1 + len(others)),
        out_specs=HBM,
        input_output_aliases={0: 0},
        compiler_params=grant(1),
        cost_estimate=cost(0.1),
        name="after",
    )(value, *others)


def run_layers(members, biases, home, partner, bundles):
    count = len(bundles)
    done = jax.ShapeDtypeStruct((2 * SLOT_ROWS, BLOCK), jnp.bfloat16)
    return pl.pallas_call(
        lambda *refs: layers_kernel(count, *refs),
        out_shape=[done] * count,
        in_specs=[SMEM, VMEM, HBM, HBM] + [HBM] * count,
        out_specs=[HBM] * count,
        scratch_shapes=[
            pltpu.VMEM((2, LAYERS, 16, 256, 128), jnp.bfloat16),
            pltpu.VMEM((2 * count + 1, SLOT_ROWS, BLOCK), jnp.bfloat16),
            pltpu.VMEM((count, TAG_ROWS, BLOCK), jnp.bfloat16),
            pltpu.SMEM((2 * count + WIDTH,), jnp.int32),
            pltpu.SMEM((2 * count + 1,), jnp.int32),
            pltpu.SemaphoreType.DMA((3 * count + 2,)),
        ]
        + [pltpu.VMEM((SLOT_ROWS, BLOCK), jnp.bfloat16)] * (2 * WIDTH),
        compiler_params=grant(20),
        cost_estimate=cost(6),
        name="layers",
    )(members, biases, home, partner, *bundles)


def shards(activations, weight_tiles, tile_index, bias_terms, demand):
    device = lax.axis_index(AXES).astype(jnp.int32).reshape(1)
    sent = jax.ShapeDtypeStruct((SENT_ROWS, BLOCK), jnp.bfloat16)

    tiles, *outgoing = pl.pallas_call(
        pack_kernel,
        out_shape=[jax.ShapeDtypeStruct(weight_tiles.shape, weight_tiles.dtype)] + [sent] * len(MOVES),
        in_specs=[SMEM, SMEM, HBM, HBM],
        out_specs=[HBM] * (1 + len(MOVES)),
        scratch_shapes=PLACE_SCRATCH
        + [pltpu.VMEM((len(MOVES), TAG_ROWS, BLOCK), jnp.bfloat16), pltpu.SemaphoreType.DMA((2 + len(MOVES),))],
        compiler_params=grant(4),
        cost_estimate=cost(4),
        name="pack",
    )(device, demand, in_hbm(weight_tiles), activations)
    arrived = [send(v, move, False) for v, move in zip(outgoing, MOVES)]
    near = after(shifted(tiles, dz=4), *arrived[:5])
    home, partner = [
        in_hbm(lax.all_gather(w, ("x", "c"), axis=1, tiled=True).reshape(LAYERS, 16, 256, 128)) for w in (weight_tiles, near)
    ]

    own_range = lax.axis_index(("z", "y"))
    ranges = [own_range, (own_range + NZ * NY // 2) % (NZ * NY)]
    members = jnp.stack(
        [lax.dynamic_slice_in_dim(tile_index[:, :, 0], r * 16, 16, 1) % CAP for r in ranges]
    )
    biases = jnp.stack(
        [lax.dynamic_slice_in_dim(bias_terms, r * 16 * BLOCK, 16 * BLOCK, 1).reshape(LAYERS, 16, BLOCK) for r in ranges]
    )

    returned = [None] * len(MOVES)
    for part in PARTS:
        results = run_layers(members, biases, home, partner, [arrived[i] for i in part])
        for i, value in zip(part, results):
            returned[i] = send(value, MOVES[i], True)

    return pl.pallas_call(
        unpack_kernel,
        out_shape=jax.ShapeDtypeStruct(activations.shape, activations.dtype),
        in_specs=[SMEM, SMEM] + [HBM] * len(MOVES),
        out_specs=HBM,
        scratch_shapes=PLACE_SCRATCH + [pltpu.SemaphoreType.DMA],
        compiler_params=grant(4),
        cost_estimate=cost(4),
        name="unpack",
    )(device, demand, *returned)


def solution(mesh):
    finer = Mesh(mesh.devices.reshape(NZ, NY, NX, NC), AXES)
    placed = (P(AXES, None), P(None, AXES, None, None, None), P(), P(), P(AXES, None))
    return jax.shard_map(
        shards, mesh=finer, in_specs=placed, out_specs=P(AXES, None), check_vma=False
    )
```

```python
import jax
import jax.numpy as jnp
from jax import lax
from jax.experimental import pallas as pl
from jax.experimental.pallas import tpu as pltpu
from jax.sharding import Mesh
from jax.sharding import PartitionSpec as P

LAYERS = 3
CAP = 4
NZ, NY, NX, NC = 8, 4, 4, 2
AXES = ("z", "y", "x", "c")
PLACES = [(z, y, x, c) for z in range(NZ) for y in range(NY) for x in range(NX) for c in range(NC)]
PLACE_ID = {place: i for i, place in enumerate(PLACES)}
MOVES = [
    *((0, 1), (0, 3), (0, 2), (1, 2), (3, 2)),
    *((1, 1), (3, 3), (2, 2), (1, 3), (3, 1)),
    *((2, 1), (2, 3), (1, 0), (3, 0), (2, 0), (0, 0)),
]
ROWS = 96
BLOCK = 128
SLOT_ROWS = CAP * ROWS
TAG_ROWS = 16
SENT_ROWS = 2 * SLOT_ROWS + TAG_ROWS
WIDTH = 4
BACK = [
    *((2, 2), (1, 1), (3, 3), (1, 3), (3, 1), (2, 1), (2, 3), (1, 2), (3, 2)),
    *((2, 0), (0, 2), (1, 0), (0, 1), (3, 0), (0, 3), (0, 0)),
]
EARLY = [0, 1, 2, 3, 4, 5, 6, 7, 8, 9, 15]


def signed(step, c):
    return {0: 0, 1: 1, 3: -1, 2: 2 - 4 * c}[step]


def permute(value, target):
    pairs = [(PLACE_ID[p], PLACE_ID[target(*p)]) for p in PLACES]
    return lax.ppermute(value, AXES, pairs)


def send(value, move, back):
    sign = -1 if back else 1

    def target(z, y, x, c):
        dz, dy = signed(move[0], c), signed(move[1], c)
        return ((z + sign * dz) % NZ, (y + sign * dy) % NY, x, c)

    return value if move == (0, 0) else permute(value, target)


def shifted(value, dz=0, dx=0, dc=0):
    return permute(value, lambda z, y, x, c: ((z + dz) % NZ, y, (x + dx) % NX, (c + dc) % NC))


def slot_range(device, move, h):
    z, y, c = device // 32, (device // 8) % 4, device % 2

    def step(s):
        return {0: 0, 1: 1, 3: 7, 2: 2 + 4 * c}[s]

    return ((z + step(move[0]) + 4 * h) % NZ) * NY + (y + step(move[1])) % NY


def note_places(demand, place, group):
    for r in range(NZ * NY):
        group[r] = -1
    for p in range(demand.shape[1]):
        block = demand[0, p]
        place[(block // 16) * CAP + block % CAP] = p
        group[block // 16] = (block // CAP) % 4


def bundle_slots(moves, device, place, group):
    for i, move in enumerate(moves):
        for h in range(2):
            r = slot_range(device, move, h)
            yield i, h, r, group[r]


def pack_kernel(device, demand, tiles, acts, tiles_out, *rest):
    outs, (place, group, tags, sems) = rest[: len(MOVES)], rest[len(MOVES) :]
    handed_on = pltpu.make_async_copy(tiles, tiles_out, sems.at[0])
    handed_on.start()
    note_places(demand, place, group)
    found = [[None, None] for _ in MOVES]
    for i, h, r, live in bundle_slots(MOVES, device[0], place, group):
        found[i][h] = live

        @pl.when(live >= 0)
        def _():
            for k in range(CAP):
                col = pl.multiple_of(place[r * CAP + k] * BLOCK, BLOCK)
                block = outs[i].at[pl.ds(h * SLOT_ROWS + k * ROWS, ROWS), :]
                pltpu.make_async_copy(acts.at[:, pl.ds(col, BLOCK)], block, sems.at[1]).start()

    line = lax.broadcasted_iota(jnp.int32, (TAG_ROWS, BLOCK), 0)
    tag_copies = []
    for i in range(len(MOVES)):
        tag = jnp.where(line < 8, found[i][0], found[i][1]).astype(jnp.float32)
        tags[i] = tag.astype(jnp.bfloat16)
        tag_copies.append(
            pltpu.make_async_copy(tags.at[i], outs[i].at[pl.ds(2 * SLOT_ROWS, TAG_ROWS), :], sems.at[2 + i])
        )
        tag_copies[-1].start()
    for copy in tag_copies:
        copy.wait()
    handed_on.wait()
    pltpu.make_async_copy(acts, acts, sems.at[1]).wait()


def unpack_kernel(device, demand, *rest):
    ins, (out, place, group, sem) = rest[: len(MOVES)], rest[len(MOVES) :]
    note_places(demand, place, group)
    for i, h, r, live in bundle_slots(BACK, device[0], place, group):

        @pl.when(live >= 0)
        def _():
            for k in range(CAP):
                col = pl.multiple_of(place[r * CAP + k] * BLOCK, BLOCK)
                block = ins[i].at[pl.ds(h * SLOT_ROWS + k * ROWS, ROWS), :]
                pltpu.make_async_copy(block, out.at[:, pl.ds(col, BLOCK)], sem).start()

    pltpu.make_async_copy(out, out, sem).wait()


def layers_kernel(jobs, sides, count, begun, members, biases, *rest):
    sources, rest = rest[: len(sides)], rest[len(sides) :]
    ins, outs, rest = rest[:count], rest[count + begun : 2 * count + begun], rest[2 * count + begun :]
    weights, slots, tags, queue, groups, flanks, sems, *states = rest
    firsts, seconds = states[:WIDTH], states[WIDTH:]
    spare = len(jobs)
    used = sorted({i for i, _ in jobs})
    copies = []
    for i in used:
        copies.append(pltpu.make_async_copy(ins[i].at[pl.ds(2 * SLOT_ROWS, TAG_ROWS), :], tags.at[i], sems.at[i]))
    for at, source in enumerate(sources):
        copies.append(pltpu.make_async_copy(source, weights.at[at], sems.at[count + at]))
    for s, (i, h) in enumerate(jobs):
        block = ins[i].at[pl.ds(h * SLOT_ROWS, SLOT_ROWS), :]
        copies.append(pltpu.make_async_copy(block, slots.at[s], sems.at[count + 2 + s]))
    for copy in copies:
        copy.start()
    for copy in copies[: len(used)]:
        copy.wait()
    found = []
    for i, h in jobs:
        tag = tags[i].astype(jnp.float32)
        found.append(jnp.max(tag[8 * h : 8 * h + 8]).astype(jnp.int32))
    live = jnp.int32(0)
    for s, (i, h) in enumerate(jobs):
        queue[live] = s
        groups[s] = jnp.maximum(found[s], 0)
        flanks[s] = h
        live = live + (found[s] >= 0).astype(jnp.int32)
    groups[spare] = 0
    flanks[spare] = sides[0]
    for u in range(WIDTH):
        queue[live + u] = spare
    for copy in copies[len(used) :]:
        copy.wait()

    def several(turn, carry):
        picked = [queue[turn * WIDTH + u] for u in range(WIDTH)]
        group = [groups[s] for s in picked]
        side = [flanks[s] for s in picked]
        for layer in range(LAYERS):
            for u in range(WIDTH):
                src = (slots.at[picked[u]], firsts[u], seconds[u])[layer]
                dst = (firsts[u], seconds[u], slots.at[picked[u]])[layer]
                for k in range(CAP):
                    block = group[u] * CAP + k
                    peer = members[side[u], layer, block]
                    own = src[pl.ds(k * ROWS, ROWS), :]
                    off = src[pl.ds(pl.multiple_of(peer * ROWS, 16), ROWS), :]
                    total = jnp.dot(
                        jnp.concatenate([own, off], axis=1),
                        weights[side[u] - sides[0], layer, block],
                        preferred_element_type=jnp.float32,
                    )
                    total = total + biases[side[u], layer, pl.ds(block, 1), :]
                    dst[pl.ds(k * ROWS, ROWS), :] = jnp.maximum(total, 0).astype(jnp.bfloat16)
        return carry

    lax.fori_loop(0, (live + WIDTH - 1) // WIDTH, several, 0)
    copies = []
    for s, (i, h) in enumerate(jobs):
        block = outs[i].at[pl.ds(h * SLOT_ROWS, SLOT_ROWS), :]
        copies.append(pltpu.make_async_copy(slots.at[s], block, sems.at[count + 2 + s]))
    for copy in copies:
        copy.start()
    for copy in copies:
        copy.wait()


SMEM = pl.BlockSpec(memory_space=pltpu.SMEM)
VMEM = pl.BlockSpec(memory_space=pltpu.VMEM)
HBM = pl.BlockSpec(memory_space=pltpu.HBM)
PLACE_SCRATCH = [pltpu.SMEM((128,), jnp.int32), pltpu.SMEM((32,), jnp.int32)]


def cost(microseconds):
    return pl.CostEstimate(flops=0, bytes_accessed=int(microseconds * 3e6), transcendentals=0)


def grant(mebibytes):
    return pltpu.CompilerParams(vmem_limit_bytes=mebibytes * 1024 * 1024)


def in_hbm(value):
    return pltpu.with_memory_space_constraint(value, pltpu.HBM)


def after(value, *others):
    return pl.pallas_call(
        lambda *refs: None,
        out_shape=jax.ShapeDtypeStruct(value.shape, value.dtype),
        in_specs=[HBM] * (1 + len(others)),
        out_specs=HBM,
        input_output_aliases={0: 0},
        compiler_params=grant(1),
        cost_estimate=cost(0.1),
        name="after",
    )(value, *others)


def run_layers(jobs, members, biases, sources, bundles, begun):
    sides = sorted(sources)
    count = len(bundles)
    done = pltpu.HBM((2 * SLOT_ROWS, BLOCK), jnp.bfloat16)
    before = 2 + len(sides) + count
    return pl.pallas_call(
        lambda *refs: layers_kernel(jobs, sides, count, len(begun), *refs),
        out_shape=[done] * count,
        in_specs=[SMEM, VMEM] + [HBM] * (len(sides) + count + len(begun)),
        out_specs=[HBM] * count,
        input_output_aliases={before + at: i for at, i in enumerate(begun)},
        scratch_shapes=[
            pltpu.VMEM((len(sides), LAYERS, 16, 256, 128), jnp.bfloat16),
            pltpu.VMEM((len(jobs) + 1, SLOT_ROWS, BLOCK), jnp.bfloat16),
            pltpu.VMEM((count, TAG_ROWS, BLOCK), jnp.bfloat16),
            pltpu.SMEM((len(jobs) + WIDTH,), jnp.int32),
            pltpu.SMEM((len(jobs) + 1,), jnp.int32),
            pltpu.SMEM((len(jobs) + 1,), jnp.int32),
            pltpu.SemaphoreType.DMA((count + 2 + len(jobs),)),
        ]
        + [pltpu.VMEM((SLOT_ROWS, BLOCK), jnp.bfloat16)] * (2 * WIDTH),
        compiler_params=grant(20),
        cost_estimate=cost(8),
        name="layers",
    )(members, biases, *[sources[h] for h in sides], *bundles, *map(in_hbm, begun.values()))


def shards(activations, weight_tiles, tile_index, bias_terms, demand):
    device = lax.axis_index(AXES).astype(jnp.int32).reshape(1)
    sent = jax.ShapeDtypeStruct((SENT_ROWS, BLOCK), jnp.bfloat16)

    tiles, *outgoing = pl.pallas_call(
        pack_kernel,
        out_shape=[jax.ShapeDtypeStruct(weight_tiles.shape, weight_tiles.dtype)] + [sent] * len(MOVES),
        in_specs=[SMEM, SMEM, HBM, HBM],
        out_specs=[HBM] * (1 + len(MOVES)),
        scratch_shapes=PLACE_SCRATCH
        + [pltpu.VMEM((len(MOVES), TAG_ROWS, BLOCK), jnp.bfloat16), pltpu.SemaphoreType.DMA((2 + len(MOVES),))],
        compiler_params=grant(4),
        cost_estimate=cost(4),
        name="pack",
    )(device, demand, in_hbm(weight_tiles), activations)
    arrived = [send(v, move, False) for v, move in zip(outgoing, MOVES)]
    near = after(shifted(tiles, dz=4), *arrived[:4])
    home, partner = [
        in_hbm(lax.all_gather(w, ("x", "c"), axis=1, tiled=True).reshape(LAYERS, 16, 256, 128)) for w in (weight_tiles, near)
    ]

    own_range = lax.axis_index(("z", "y"))
    ranges = [own_range, (own_range + NZ * NY // 2) % (NZ * NY)]
    members = jnp.stack(
        [lax.dynamic_slice_in_dim(tile_index[:, :, 0], r * 16, 16, 1) % CAP for r in ranges]
    )
    biases = jnp.stack(
        [lax.dynamic_slice_in_dim(bias_terms, r * 16 * BLOCK, 16 * BLOCK, 1).reshape(LAYERS, 16, BLOCK) for r in ranges]
    )

    jobs = [(at, 0) for at in range(len(EARLY))]
    begun = run_layers(jobs, members, biases, {0: home}, [arrived[i] for i in EARLY], {})
    jobs = [(i, h) for i in range(len(MOVES)) for h in range(2) if h or i not in EARLY]
    results = run_layers(jobs, members, biases, {0: home, 1: partner}, arrived, dict(zip(EARLY, begun)))
    returned = [send(results[MOVES.index(move)], move, True) for move in BACK]

    return pl.pallas_call(
        unpack_kernel,
        out_shape=jax.ShapeDtypeStruct(activations.shape, activations.dtype),
        in_specs=[SMEM, SMEM] + [HBM] * len(MOVES),
        out_specs=HBM,
        scratch_shapes=PLACE_SCRATCH + [pltpu.SemaphoreType.DMA],
        compiler_params=grant(4),
        cost_estimate=cost(4),
        name="unpack",
    )(device, demand, *returned)


def solution(mesh):
    finer = Mesh(mesh.devices.reshape(NZ, NY, NX, NC), AXES)
    placed = (P(AXES, None), P(None, AXES, None, None, None), P(), P(), P(AXES, None))
    return jax.shard_map(
        shards, mesh=finer, in_specs=placed, out_specs=P(AXES, None), check_vma=False
    )
```

```python
import jax
import jax.numpy as jnp
from jax import lax
from jax.experimental import pallas as pl
from jax.experimental.pallas import tpu as pltpu
from jax.sharding import Mesh
from jax.sharding import PartitionSpec as P

LAYERS = 3
CAP = 4
NZ, NY, NX, NC = 8, 4, 4, 2
AXES = ("z", "y", "x", "c")
PLACES = [(z, y, x, c) for z in range(NZ) for y in range(NY) for x in range(NX) for c in range(NC)]
PLACE_ID = {place: i for i, place in enumerate(PLACES)}
Z_MOVES = [
    *((1, 2), (3, 2), (1, 1), (3, 3), (2, 2), (1, 3), (3, 1)),
    *((2, 1), (2, 3), (2, 0), (1, 0), (3, 0)),
]
Y_MOVES = [(0, dy) for dy in range(NY)]
MOVES = Z_MOVES + Y_MOVES
BACK = [
    *((2, 2), (1, 1), (3, 3), (1, 3), (3, 1), (2, 1), (2, 3)),
    *((1, 2), (3, 2), (2, 0), (1, 0), (3, 0)),
]
EARLY = [*Z_MOVES[:8], *Y_MOVES]
ROWS = 96
BLOCK = 128
SLOT_ROWS = CAP * ROWS
TAG_ROWS = 16
SENT_ROWS = 2 * SLOT_ROWS + TAG_ROWS
WIDTH = 4
TIED = Y_MOVES[1:]


def signed(step, c):
    return {0: 0, 1: 1, 3: -1, 2: 2 - 4 * c}[step]


def permute(value, target):
    pairs = [(PLACE_ID[p], PLACE_ID[target(*p)]) for p in PLACES]
    return lax.ppermute(value, AXES, pairs)


def send(value, move, back):
    sign = -1 if back else 1

    def target(z, y, x, c):
        dz, dy = signed(move[0], c), signed(move[1], c)
        return ((z + sign * dz) % NZ, (y + sign * dy) % NY, x, c)

    return value if move == (0, 0) else permute(value, target)


def shifted(value, dz=0, dx=0, dc=0):
    return permute(value, lambda z, y, x, c: ((z + dz) % NZ, y, (x + dx) % NX, (c + dc) % NC))


def slot_range(device, move, h):
    z, y, c = device // 32, (device // 8) % 4, device % 2

    def step(s):
        return {0: 0, 1: 1, 3: 7, 2: 2 + 4 * c}[s]

    return ((z + step(move[0]) + 4 * h) % NZ) * NY + (y + step(move[1])) % NY


def note_places(demand, place, group):
    for r in range(NZ * NY):
        group[r] = -1
    for p in range(demand.shape[1]):
        block = demand[0, p]
        place[(block // 16) * CAP + block % CAP] = p
        group[block // 16] = (block // CAP) % 4


def back_refs(refs, moves, device, sign):
    alone = [move for move in moves if move in Z_MOVES]
    views = dict(zip(alone, refs))
    for move in moves[len(alone) :]:
        views[move] = refs[len(alone)].at[(device // 8 + sign * move[1] + NY) % NY]
    return views


def arrays_of(moves):
    alone = sum(move in Z_MOVES for move in moves)
    return alone + (alone < len(moves))


def bundle_slots(moves, device, place, group):
    for move in moves:
        for h in range(2):
            r = slot_range(device, move, h)
            yield move, h, r, group[r]


def pack_kernel(device, demand, acts, *rest):
    outs, (place, group, tags, sems) = dict(zip(MOVES, rest)), rest[len(MOVES) :]
    note_places(demand, place, group)
    found = {move: [None, None] for move in MOVES}
    for move, h, r, live in bundle_slots(MOVES, device[0], place, group):
        found[move][h] = live

        @pl.when(live >= 0)
        def _():
            for k in range(CAP):
                col = pl.multiple_of(place[r * CAP + k] * BLOCK, BLOCK)
                block = outs[move].at[pl.ds(h * SLOT_ROWS + k * ROWS, ROWS), :]
                pltpu.make_async_copy(acts.at[:, pl.ds(col, BLOCK)], block, sems.at[0]).start()

    line = lax.broadcasted_iota(jnp.int32, (TAG_ROWS, BLOCK), 0)
    tag_copies = []
    for i, move in enumerate(MOVES):
        tag = jnp.where(line < 8, found[move][0], found[move][1]).astype(jnp.float32)
        tags[i] = tag.astype(jnp.bfloat16)
        tag_copies.append(
            pltpu.make_async_copy(tags.at[i], outs[move].at[pl.ds(2 * SLOT_ROWS, TAG_ROWS), :], sems.at[1 + i])
        )
        tag_copies[-1].start()
    for copy in tag_copies:
        copy.wait()
    pltpu.make_async_copy(acts, acts, sems.at[0]).wait()


def unpack_kernel(device, demand, *rest):
    count = arrays_of(MOVES)
    ins, (out, place, group, sem) = rest[:count], rest[count:]
    ins = back_refs(ins, MOVES, device[0], 1)
    note_places(demand, place, group)
    for move, h, r, live in bundle_slots(MOVES, device[0], place, group):

        @pl.when(live >= 0)
        def _():
            for k in range(CAP):
                col = pl.multiple_of(place[r * CAP + k] * BLOCK, BLOCK)
                block = ins[move].at[pl.ds(h * SLOT_ROWS + k * ROWS, ROWS), :]
                pltpu.make_async_copy(block, out.at[:, pl.ds(col, BLOCK)], sem).start()

    pltpu.make_async_copy(out, out, sem).wait()


def layers_kernel(jobs, moves, sides, carried, begun, device, members, biases, *rest):
    fresh = [move for move in moves if move not in carried]
    count = len(fresh)
    gone = arrays_of(moves)
    given = sum(2 - h for h in sides)
    sources, rest = rest[:given], rest[given:]
    ins, outs, rest = rest[:count], rest[count + begun : count + begun + gone], rest[count + begun + gone :]
    weights, slots, tags, queue, groups, flanks, sems, *states = rest
    firsts, seconds = states[:WIDTH], states[WIDTH:]
    spare = len(jobs)
    outs = back_refs(outs, moves, device[0], -1)
    ins = dict(zip(fresh, ins)) | {move: outs[move] for move in carried}
    base = len(moves)
    copies = []
    for i, move in enumerate(moves):
        copies.append(pltpu.make_async_copy(ins[move].at[pl.ds(2 * SLOT_ROWS, TAG_ROWS), :], tags.at[i], sems.at[i]))
    x, c = (device[0] // 2) % NX, device[0] % NC
    if 0 in sides:
        for core in range(NC):
            for step in range(NX):
                spot = (x + step) % NX * NC + (c + core) % NC
                copies.append(
                    pltpu.make_async_copy(sources[core].at[step], weights.at[0, spot], sems.at[base + NX * core + step])
                )
    if 1 in sides:
        copies.append(pltpu.make_async_copy(sources[-1], weights.at[len(sides) - 1], sems.at[base + 8]))
    for s, (move, h) in enumerate(jobs):
        block = ins[move].at[pl.ds(h * SLOT_ROWS, SLOT_ROWS), :]
        copies.append(pltpu.make_async_copy(block, slots.at[s], sems.at[base + 9 + s]))
    passed_on = []
    for i, move in enumerate(moves if not carried else []):
        there = pl.ds(SLOT_ROWS, SLOT_ROWS + TAG_ROWS)
        passed_on.append(
            pltpu.make_async_copy(ins[move].at[there, :], outs[move].at[there, :], sems.at[base + 9 + len(jobs) + i])
        )
    for copy in copies + passed_on:
        copy.start()
    for copy in copies[:base]:
        copy.wait()
    found = []
    for move, h in jobs:
        tag = tags[moves.index(move)].astype(jnp.float32)
        found.append(jnp.max(tag[8 * h : 8 * h + 8]).astype(jnp.int32))
    live = jnp.int32(0)
    for s, (move, h) in enumerate(jobs):
        queue[live] = s
        groups[s] = jnp.maximum(found[s], 0)
        flanks[s] = h
        live = live + (found[s] >= 0).astype(jnp.int32)
    groups[spare] = 0
    flanks[spare] = sides[0]
    for u in range(WIDTH):
        queue[live + u] = spare
    for copy in copies[base:]:
        copy.wait()

    def several(turn, carry):
        picked = [queue[turn * WIDTH + u] for u in range(WIDTH)]
        group = [groups[s] for s in picked]
        side = [flanks[s] for s in picked]
        for layer in range(LAYERS):
            for u in range(WIDTH):
                src = (slots.at[picked[u]], firsts[u], seconds[u])[layer]
                dst = (firsts[u], seconds[u], slots.at[picked[u]])[layer]
                for k in range(CAP):
                    block = group[u] * CAP + k
                    peer = members[side[u], layer, block]
                    own = src[pl.ds(k * ROWS, ROWS), :]
                    off = src[pl.ds(pl.multiple_of(peer * ROWS, 16), ROWS), :]
                    total = jnp.dot(
                        jnp.concatenate([own, off], axis=1),
                        weights[side[u] - sides[0], group[u] * NC + k // 2, layer, k % 2],
                        preferred_element_type=jnp.float32,
                    )
                    total = total + biases[side[u], layer, pl.ds(block, 1), :]
                    dst[pl.ds(k * ROWS, ROWS), :] = jnp.maximum(total, 0).astype(jnp.bfloat16)
        return carry

    lax.fori_loop(0, (live + WIDTH - 1) // WIDTH, several, 0)
    copies = []
    for s, (move, h) in enumerate(jobs):
        block = outs[move].at[pl.ds(h * SLOT_ROWS, SLOT_ROWS), :]
        copies.append(pltpu.make_async_copy(slots.at[s], block, sems.at[base + 9 + s]))
    for copy in copies:
        copy.start()
    for copy in copies + passed_on:
        copy.wait()


SMEM = pl.BlockSpec(memory_space=pltpu.SMEM)
VMEM = pl.BlockSpec(memory_space=pltpu.VMEM)
HBM = pl.BlockSpec(memory_space=pltpu.HBM)
PLACE_SCRATCH = [pltpu.SMEM((128,), jnp.int32), pltpu.SMEM((32,), jnp.int32)]


def cost(microseconds):
    return pl.CostEstimate(flops=0, bytes_accessed=int(microseconds * 3e6), transcendentals=0)


def grant(mebibytes):
    return pltpu.CompilerParams(vmem_limit_bytes=mebibytes * 1024 * 1024)


def in_hbm(value):
    return pltpu.with_memory_space_constraint(value, pltpu.HBM)


def after(value, *others):
    return pl.pallas_call(
        lambda *refs: None,
        out_shape=jax.ShapeDtypeStruct(value.shape, value.dtype),
        in_specs=[HBM] * (1 + len(others)),
        out_specs=HBM,
        input_output_aliases={0: 0},
        compiler_params=grant(1),
        cost_estimate=cost(0.1),
        name="after",
    )(value, *others)


def shapes_of(moves, rows, make):
    alone = sum(move in Z_MOVES for move in moves)
    shapes = [make((rows, BLOCK), jnp.bfloat16)] * alone
    return shapes + [make((NY, rows, BLOCK), jnp.bfloat16)] * (arrays_of(moves) - alone)


def run_layers(jobs, moves, device, members, biases, sources, bundles, carried, begun):
    sides = sorted(sources)
    done = shapes_of(moves, SENT_ROWS, pltpu.HBM)
    given = [part for h in sides for part in sources[h]]
    before = 3 + len(given) + len(bundles)
    return pl.pallas_call(
        lambda *refs: layers_kernel(jobs, moves, sides, carried, len(begun), *refs),
        out_shape=done,
        in_specs=[SMEM, SMEM, VMEM] + [HBM] * (len(given) + len(bundles) + len(begun)),
        out_specs=[HBM] * len(done),
        input_output_aliases={before + at: i for at, i in enumerate(begun)},
        scratch_shapes=[
            pltpu.VMEM((len(sides), NX * NC, LAYERS, 2, 256, 128), jnp.bfloat16),
            pltpu.VMEM((len(jobs) + 1, SLOT_ROWS, BLOCK), jnp.bfloat16),
            pltpu.VMEM((len(moves), TAG_ROWS, BLOCK), jnp.bfloat16),
            pltpu.SMEM((len(jobs) + WIDTH,), jnp.int32),
            pltpu.SMEM((len(jobs) + 1,), jnp.int32),
            pltpu.SMEM((len(jobs) + 1,), jnp.int32),
            pltpu.SemaphoreType.DMA((2 * len(moves) + 9 + len(jobs),)),
        ]
        + [pltpu.VMEM((SLOT_ROWS, BLOCK), jnp.bfloat16)] * (2 * WIDTH),
        compiler_params=grant(20),
        cost_estimate=cost(8),
        name="layers",
    )(device, members, biases, *given, *(map(in_hbm, bundles) if carried else bundles), *map(in_hbm, begun.values()))


def shards(activations, weight_tiles, tile_index, bias_terms, demand):
    device = lax.axis_index(AXES).astype(jnp.int32).reshape(1)
    sent = [pltpu.HBM((SENT_ROWS, BLOCK), jnp.bfloat16)] * len(MOVES)

    outgoing = pl.pallas_call(
        pack_kernel,
        out_shape=sent,
        in_specs=[SMEM, SMEM, HBM],
        out_specs=[HBM] * len(sent),
        scratch_shapes=PLACE_SCRATCH
        + [pltpu.VMEM((len(MOVES), TAG_ROWS, BLOCK), jnp.bfloat16), pltpu.SemaphoreType.DMA((1 + len(MOVES),))],
        compiler_params=grant(4),
        cost_estimate=cost(4),
        name="pack",
    )(device, demand, activations)
    arrived = {move: send(v, move, False) for v, move in zip(outgoing, MOVES)}
    tiles = weight_tiles.reshape(LAYERS, 2, 256, 128)

    def gathered(value):
        copies = jnp.broadcast_to(value, (NX * NC, *value.shape))
        return in_hbm(lax.all_to_all(copies, ("x", "c"), 0, 0, tiled=True))

    mine = jnp.stack([tiles, *[shifted(tiles, dx=step) for step in (-1, 2, 1)]])
    home = [in_hbm(mine), in_hbm(shifted(mine, dc=1))]
    near = after(shifted(tiles, dz=4), mine, *[arrived[move] for move in TIED])
    partner = [gathered(near)]

    own_range = lax.axis_index(("z", "y"))
    ranges = [own_range, (own_range + NZ * NY // 2) % (NZ * NY)]
    members = jnp.stack(
        [lax.dynamic_slice_in_dim(tile_index[:, :, 0], r * 16, 16, 1) % CAP for r in ranges]
    )
    biases = jnp.stack(
        [lax.dynamic_slice_in_dim(bias_terms, r * 16 * BLOCK, 16 * BLOCK, 1).reshape(LAYERS, 16, BLOCK) for r in ranges]
    )

    first = [at for at, move in enumerate(Z_MOVES) if move in EARLY] + [len(Z_MOVES)]
    jobs = [(move, 0) for move in EARLY]
    begun = run_layers(jobs, EARLY, device, members, biases, {0: home}, [arrived[move] for move in EARLY], [], {})
    jobs = [(move, h) for move in MOVES for h in range(2) if h or move not in EARLY]
    late = [arrived[move] for move in MOVES if move not in EARLY]
    results = run_layers(
        jobs, MOVES, device, members, biases, {0: home, 1: partner}, late, EARLY, dict(zip(first, begun))
    )
    returned = {(0, 0): lax.all_to_all(results[-1], "y", 0, 0, tiled=True)}
    for move in BACK:
        returned[move] = send(results[Z_MOVES.index(move)], move, True)
    returned = [returned[move] for move in Z_MOVES] + [returned[0, 0]]

    return pl.pallas_call(
        unpack_kernel,
        out_shape=jax.ShapeDtypeStruct(activations.shape, activations.dtype),
        in_specs=[SMEM, SMEM] + [HBM] * len(returned),
        out_specs=HBM,
        scratch_shapes=PLACE_SCRATCH + [pltpu.SemaphoreType.DMA],
        compiler_params=grant(4),
        cost_estimate=cost(4),
        name="unpack",
    )(device, demand, *returned)


def solution(mesh):
    finer = Mesh(mesh.devices.reshape(NZ, NY, NX, NC), AXES)
    placed = (P(AXES, None), P(None, AXES, None, None, None), P(), P(), P(AXES, None))
    return jax.shard_map(
        shards, mesh=finer, in_specs=placed, out_specs=P(AXES, None), check_vma=False
    )
```
